128 devices in a mesh: frag: 8 (over x, core), grid: 16 (over y, z).
Axes of the slice: x: 4, y: 4, z: 4, core: 2. Of those that a mesh axis runs over, the one named last changes fastest.
Arguments:
- kinetic: bfloat16 [256, 1024, 1024], P(('frag', 'grid')), may hold values from -1 to 4, as said below
- basis: bfloat16 [256, 2048, 1024], P(('frag', 'grid')), may hold values from -0.1875 to 0.1875
- start_orbitals: bfloat16 [256, 1024, 128], P(('frag', 'grid')), may hold values from -6 to 6
- background: float32 [256, 256, 256], P('frag', 'grid'), may hold values from -2 to 2
- tile_ids: int32 [256, 8], P(('frag', 'grid')), may hold values from 0 to 65535, as said below
- tile_counts: int32 [256], P(('frag', 'grid')), may hold values from 6 to 8, as said below
- degrees: int32 [256], P(('frag', 'grid')), may hold values from 1 to 2
Outputs:
- potential: float32 [256, 256, 256], P('frag', 'grid')
- density_out: float32 [256, 256, 256], P('frag', 'grid')
The draws below stay inside these ranges and needn't reach their ends.
Inputs may be any that keep to these rules, and one draw needn't show every extreme that they name: `kinetic`: each fragment's matrix is symmetric. `tile_ids`: fragments lie 2 to a device in the order of frag+grid. A fragment's live lines are distinct, and their x lies in the block of 32 planes of the fragment's index of frag. Among the live lines of one device's fragments at most 2 have y in any one block of 16 rows, and on every device exactly 2 do for some block. `tile_counts`: every device holds a fragment with 8 live tiles.
All inputs are finite; a program needn't handle non-finite values.
Results may differ from the reference program's by a relative error of at most 0.002.
Values sent between devices are 32-bit elements; how exact they have to be, the bound alone decides.
No kernel may reach another device: no remote copies, remote signals or barrier semaphores. Data moves between devices by JAX's collectives and lax.ppermute only.
A program may use at most 128 MiB of HBM per device.

```python
import jax
import jax.numpy as jnp
from jax import lax

NX = 256
NY = 256
NZ = 256
NB = 1024
M = 128
FRAG_DEV = 2
TMAX = 8
DEG = 2
STEPS = 2
FRAGS = 256
CX = 32
CY = 16
N_FRAG = 8
N_GRID = 16


def layout_draw(key):
    devices = N_FRAG * N_GRID
    entries = FRAG_DEV * TMAX
    pool = 2 * N_GRID
    keys = jax.random.split(jax.random.fold_in(key, 101), devices)

    def one_device(device_key, device):
        parts = jax.random.split(device_key, 8)
        counts = jax.random.randint(parts[0], (FRAG_DEV,), max(TMAX - 2, 1), TMAX + 1)
        fullest = jax.random.randint(parts[1], (), 0, FRAG_DEV)
        counts = jnp.where(jnp.arange(FRAG_DEV) == fullest, TMAX, counts)
        sequence = jax.random.permutation(parts[2], pool) % N_GRID
        place = jnp.arange(pool)
        dropped = (place == 0) | (sequence == sequence[0]) & (place > 0)
        remaining = sequence[jnp.argsort(dropped.astype(jnp.int32), stable=True)]
        first_slot = jax.random.randint(parts[3], (), 0, TMAX)
        second_slot = (first_slot + 1 + jax.random.randint(parts[4], (), 0, TMAX - 1)) % TMAX
        position = jnp.arange(entries)
        paired = (position == fullest * TMAX + first_slot) | (position == fullest * TMAX + second_slot)
        order = jnp.cumsum(1 - paired.astype(jnp.int32)) - 1
        owner = jnp.where(paired, sequence[0], remaining[jnp.clip(order, 0, pool - 3)])
        base = jax.random.randint(parts[5], (entries,), 0, CY)
        before = (owner[:, None] == owner[None, :]) & (position[None, :] < position[:, None])
        has_before = jnp.any(before, axis=1)
        partner = jnp.sum(jnp.where(before, base[None, :], 0), axis=1)
        shift = 1 + jax.random.randint(parts[6], (entries,), 0, CY - 1)
        offset = jnp.where(has_before, (partner + shift) % CY, base)
        plane = device // N_GRID * CX + jax.random.randint(parts[7], (entries,), 0, CX)
        lines = plane * NY + owner * CY + offset
        return (lines.reshape(FRAG_DEV, TMAX).astype(jnp.int32), counts.astype(jnp.int32))
    lines, counts = jax.vmap(one_device)(keys, jnp.arange(devices))
    return (lines.reshape(FRAG_DEV * devices, TMAX), counts.reshape(-1))


def draw_tile_ids(key, part):
    return layout_draw(key)[0]


def draw_tile_counts(key, part):
    return layout_draw(key)[1]


def draw_kinetic(key, part):
    keys = jax.random.split(jax.random.fold_in(key, 202), FRAGS)

    def one_fragment(fragment_key):
        noise_key, diagonal_key = jax.random.split(fragment_key)
        noise = jax.random.normal(noise_key, (NB, NB), jnp.float32)
        mirror = (noise + noise.T) * 0.5 ** 0.5 * NB ** (-0.5)
        diagonal = jax.random.uniform(diagonal_key, (NB,), jnp.float32, 0.5, 4.0)
        identity = jnp.eye(NB, dtype=jnp.float32)
        return (mirror * (1.0 - identity) + identity * diagonal[:, None]).astype(jnp.bfloat16)
    return lax.map(one_fragment, keys)


def place_ends(values, own_key, smallest, top_value):
    extent = values.shape
    spot = [jax.random.randint(jax.random.fold_in(own_key, axis), (), 0, extent[axis]) for axis in range(len(extent))]
    values = values.at[tuple(spot)].set(smallest)
    longest = extent.index(max(extent))
    spot[longest] = (spot[longest] + 1) % extent[longest]
    return values.at[tuple(spot)].set(top_value)


def level_of(key, dims, cuts, least, top_value):
    def one(axis_at, shards_of):
        draws = jax.random.uniform(jax.random.fold_in(jax.random.fold_in(key, 6), axis_at), (shards_of,), jnp.float32, least / len(cuts), top_value / len(cuts))
        return jnp.repeat(jnp.exp(draws), dims[axis_at] // shards_of).reshape((-1,) + (1,) * (len(dims) - axis_at - 1))

    level = one(*cuts[0])
    for cut in cuts[1:]:
        level = level * one(*cut)
    return level


def scatter_about(own_key, shape, width, bound, cuts=(), kind=jnp.bfloat16):
    result = jax.random.normal(own_key, shape, jnp.float32) * width
    if len(cuts) > 0:
        result = level_of(own_key, shape, cuts, -0.22, 0.18) * result
    return jnp.clip(result, min=-bound, max=bound).astype(kind)


def setup_inputs(seed: int = 0) -> dict:
    key_list = jax.random.split(jax.random.key(seed), 8)
    kinetic = draw_kinetic(jax.random.fold_in(key_list[7], 71), 0)
    basis = scatter_about(key_list[1], (FRAGS, TMAX * NZ, NB), NB ** -0.5, 0.1875, ((0, 128),))
    start_orbitals = scatter_about(key_list[2], (FRAGS, NB, M), 1.0, 6.0, ((0, 128),))
    background = scatter_about(key_list[3], (NX, NY, NZ), 0.3, 2.0, ((0, 8), (1, 16)), jnp.float32)
    tile_ids = draw_tile_ids(jax.random.fold_in(key_list[7], 71), 0)
    tile_counts = draw_tile_counts(jax.random.fold_in(key_list[7], 71), 0)
    degrees = place_ends(jax.random.randint(key_list[6], (FRAGS,), 1, DEG + 1), jax.random.fold_in(key_list[6], 1), 1, DEG).astype(jnp.int32)
    return {"kinetic": kinetic, "basis": basis, "start_orbitals": start_orbitals, "background": background, "tile_ids": tile_ids, "tile_counts": tile_counts, "degrees": degrees}


filter_center = 5.0
filter_half = 4.0
full_precision = lax.Precision.HIGHEST

def sine_rows(row_index, length):
    column = jnp.arange(length, dtype=jnp.int32) + 1
    phase = (row_index + 1)[:, None] * column[None, :] % (2 * (length + 1))
    angle = jnp.pi * phase.astype(jnp.float32) / (length + 1)
    return jnp.sqrt(jnp.float32(2.0 / (length + 1))) * jnp.sin(angle)

def eigen_line(row_index, length):
    return 2.0 - 2.0 * jnp.cos(jnp.pi * (row_index + 1).astype(jnp.float32) / (length + 1))

def orthonormalize(block):
    gram = jnp.dot(block.T, block, precision=full_precision)
    factor = jnp.linalg.cholesky(gram)
    return jax.scipy.linalg.solve_triangular(factor, block.T, lower=True).T

def apply_hamiltonian(kinetic_f, basis_f, field_f, vector):
    collocated = jnp.dot(basis_f.astype(jnp.float32), vector.astype(jnp.float32), preferred_element_type=jnp.float32)
    weighted = (field_f[:, None] * collocated).astype(jnp.bfloat16)
    local_part = jnp.dot(kinetic_f.astype(jnp.float32), vector.astype(jnp.float32), preferred_element_type=jnp.float32)
    grid_part = jnp.dot(basis_f.T.astype(jnp.float32), weighted.astype(jnp.float32), preferred_element_type=jnp.float32)
    return local_part + grid_part

def filter_step(item):
    kinetic_f, basis_f, field_f, degree, orbitals = item
    earlier = orbitals.astype(jnp.bfloat16)
    current = (apply_hamiltonian(kinetic_f, basis_f, field_f, earlier) - filter_center * earlier.astype(jnp.float32)) / filter_half
    chosen = current
    for order in range(2, DEG + 1):
        rounded = current.astype(jnp.bfloat16)
        following = 2.0 * (apply_hamiltonian(kinetic_f, basis_f, field_f, rounded) - filter_center * rounded.astype(jnp.float32)) / filter_half - earlier.astype(jnp.float32)
        chosen = jnp.where(degree == order, following, chosen)
        earlier, current = (rounded, following)
    return orthonormalize(chosen)

def density_rows(basis_f, orbitals):
    values = jnp.dot(basis_f.astype(jnp.float32), orbitals.astype(jnp.bfloat16).astype(jnp.float32), preferred_element_type=jnp.float32)
    return 2.0 * lax.optimization_barrier(jnp.sum(values * values, axis=1))

def solve_potential(source):
    table_x = sine_rows(jnp.arange(NX, dtype=jnp.int32), NX)
    table_y = sine_rows(jnp.arange(NY, dtype=jnp.int32), NY)
    table_z = sine_rows(jnp.arange(NZ, dtype=jnp.int32), NZ)

    def transform(field):
        field = jnp.einsum('ai,ijk->ajk', table_x, field, precision=full_precision)
        field = jnp.einsum('bj,ajk->abk', table_y, field, precision=full_precision)
        return jnp.einsum('ck,abk->abc', table_z, field, precision=full_precision)
    eigen = eigen_line(jnp.arange(NX, dtype=jnp.int32), NX)[:, None, None] + eigen_line(jnp.arange(NY, dtype=jnp.int32), NY)[None, :, None]
    eigen = eigen + eigen_line(jnp.arange(NZ, dtype=jnp.int32), NZ)[None, None, :]
    return transform(transform(source) / eigen)

def reference(kinetic, basis, start_orbitals, background, tile_ids, tile_counts, degrees):
    live = jnp.arange(TMAX, dtype=jnp.int32)[None, :] < tile_counts[:, None]
    live_rows = jnp.repeat(live.astype(jnp.float32), NZ, axis=1)
    lines = tile_ids.reshape(-1).astype(jnp.int32)

    def initial(item):
        basis_f, start_f, live_f, count_f = item
        orbitals = orthonormalize(start_f.astype(jnp.float32))
        density = density_rows(basis_f, orbitals) * live_f
        mean_value = jnp.sum(density) / (count_f * NZ).astype(jnp.float32)
        return (orbitals, (density - mean_value) * live_f)
    orbitals, charge = lax.map(initial, (basis, start_orbitals, live_rows, tile_counts))
    gathered = jnp.zeros((NX * NY, NZ), jnp.float32).at[lines].add(charge.reshape(-1, NZ))
    source = gathered.reshape(NX, NY, NZ) - background
    potential = solve_potential(source)
    field = potential.reshape(NX * NY, NZ)[lines].reshape(FRAGS, TMAX * NZ) * live_rows
    for step in range(STEPS):
        orbitals = lax.map(filter_step, (kinetic, basis, field, degrees, orbitals))
    final = lax.map(lambda item: density_rows(item[0], item[1]) * item[2], (basis, orbitals, live_rows))
    density_out = jnp.zeros((NX * NY, NZ), jnp.float32).at[lines].add(final.reshape(-1, NZ)).reshape(NX, NY, NZ)
    return (potential, density_out)
```

```python
import jax
import jax.numpy as jnp
import ml_dtypes
import numpy as np
from jax import lax
from jax.experimental import pallas as pl
from jax.experimental.pallas import tpu as pltpu
from jax.sharding import PartitionSpec as P

f32 = jnp.float32
bf16 = jnp.bfloat16

STEPS = 2
CENTER = 5.0
HALF = 4.0
FRAGS = 2
TILES = 8
ENTRIES = FRAGS * TILES
N = 256
GROUPS = 8
OWNERS = 16
PEERS = GROUPS * OWNERS
PLANES = N // GROUPS
ROWS = N // OWNERS
CELLS = PLANES * ROWS
ORB = 128
BASIS = 1024
POINTS = TILES * N
MSG = 9
BOTH = ("frag", "grid")

NN = (((1,), (0,)), ((), ()))
NT = (((1,), (1,)), ((), ()))
TN = (((0,), (0,)), ((), ()))


def sine_table():
    index = np.arange(1, N + 1)
    phase = np.outer(index, index) % (2 * (N + 1))
    return np.sqrt(2.0 / (N + 1)) * np.sin(np.pi * phase / (N + 1))


def eigen_values():
    return 4.0 * np.sin(np.pi * np.arange(1, N + 1) / (2.0 * (N + 1))) ** 2


def halves(table):
    table = table.astype(np.float32)
    high = table.astype(ml_dtypes.bfloat16)
    low = (table - high.astype(np.float32)).astype(ml_dtypes.bfloat16)
    return jnp.asarray(np.stack([high, low]))


def dot(a, b, dims=NN):
    return lax.dot_general(a, b, dims, preferred_element_type=f32)


def split(x):
    high = x.astype(bf16)
    return high, (x - high.astype(f32)).astype(bf16)


def split3(x):
    high = x.astype(bf16)
    rest = x - high.astype(f32)
    middle = rest.astype(bf16)
    return high, middle, (rest - middle.astype(f32)).astype(bf16)


def dot3(a, b, dims=NN):
    return dot(a[0], b[0], dims) + (dot(a[0], b[1], dims) + dot(a[1], b[0], dims))


def spread(x):
    return jnp.broadcast_to(x, (8, 128))


def tree_sum(terms):
    terms = list(terms)
    while len(terms) > 1:
        terms = [
            terms[i] + terms[i + 1] if i + 1 < len(terms) else terms[i]
            for i in range(0, len(terms), 2)
        ]
    return terms[0]


def eliminate(panel, k, lane, sub):
    inside = (lane >= k) & (lane < k + 8)
    column = [spread(panel[:, k + j : k + j + 1]) for j in range(8)]
    panel = jnp.where(inside, jnp.where(lane - k == sub, 1.0, 0.0), panel)
    factor = jnp.zeros((8, 128), f32)
    scale = jnp.zeros((8, 128), f32)
    for j in range(8):
        pivot = spread(column[j][j : j + 1, :])
        guess = pl.reciprocal(pivot, approx=True)
        inverse = guess * (2.0 - pivot * guess)
        row = spread(panel[j : j + 1, :])
        factor = jnp.where(sub == j, row * lax.rsqrt(pivot), factor)
        scale = jnp.where(sub == j, inverse, scale)
        ratio = jnp.where(sub == j, 0.0, column[j] * inverse)
        for i in range(j + 1, 8):
            column[i] = column[i] - ratio * spread(column[i][j : j + 1, :])
        panel = panel - ratio * row
    return jnp.where(lane < k + 8, factor, 0.0), panel * scale, inside


def inverse_factors(gram, factors):
    lane = lax.broadcasted_iota(jnp.int32, (8, 128), 1)
    sub = lax.broadcasted_iota(jnp.int32, (8, 128), 0)
    for block in range(ORB // 8):
        k = 8 * block
        for f in range(FRAGS):
            rows, solved, inside = eliminate(gram[f, k : k + 8, :], k, lane, sub)
            factors[f, k : k + 8, :] = rows
            solved_rows = [spread(solved[j : j + 1, :]) for j in range(8)]
            for q in range(block + 1, ORB // 8):
                below = gram[f, 8 * q : 8 * q + 8, :]
                update = tree_sum(
                    [spread(below[:, k + j : k + j + 1]) * solved_rows[j] for j in range(8)]
                )
                gram[f, 8 * q : 8 * q + 8, :] = jnp.where(inside, 0.0, below) - update


def line_index(ids, counts, e):
    f, t = divmod(e, TILES)
    return jnp.where(t < counts[f], ids[f, t], -1)


def live_rows(counts, f):
    slot = lax.broadcasted_iota(jnp.int32, (TILES, N), 0)
    return (slot < counts[f]).astype(f32)


def density_lines(values, lines, f):
    row = 2.0 * jnp.sum(values * values, axis=0, keepdims=True)
    for t in range(TILES):
        lines[f * TILES + t : f * TILES + t + 1, :] = row[:, t * N : (t + 1) * N]


def start_kernel(
    ids, counts, start, ground, table_z, basis, send, orbitals, collocated,
    held, sem, gram, factors, ground_high, ground_low, lines,
):
    copies = [pltpu.make_async_copy(basis.at[f], held.at[f], sem.at[f]) for f in range(FRAGS)]
    for copy in copies:
        copy.start()
    eye = (
        lax.broadcasted_iota(jnp.int32, (ORB, ORB), 0)
        == lax.broadcasted_iota(jnp.int32, (ORB, ORB), 1)
    ).astype(f32).astype(bf16)
    turned = []
    for f in range(FRAGS):
        across = dot(eye, start[f], NT).astype(bf16)
        turned.append(across)
        gram[f] = dot(across, across, NT)
    for y in range(ROWS):
        high, low = split(ground[:, y, :])
        ground_high[y * PLANES : (y + 1) * PLANES, :] = high
        ground_low[y * PLANES : (y + 1) * PLANES, :] = low
    table = (table_z[0], table_z[1])
    spectrum = dot3(table, (ground_high[...], ground_low[...]), NT)
    for z in range(2):
        for g in range(4):
            send[pl.ds(z * 4 + g, PEERS, stride=MSG), :] = spectrum[
                z * PEERS : (z + 1) * PEERS, g * 128 : (g + 1) * 128
            ]
    inverse_factors(gram, factors)
    charges = []
    for f in range(FRAGS):
        parts = split3(factors[f])
        rotated = dot(parts[0], turned[f]) + (dot(parts[1], turned[f]) + dot(parts[2], turned[f]))
        rounded = rotated.astype(bf16)
        orbitals[f] = rounded
        copies[f].wait()
        values = dot(rounded, held[f], NT)
        collocated[f] = values
        density_lines(values, lines, f)
        live = live_rows(counts, f)
        density = lines[f * TILES : (f + 1) * TILES, :] * live
        mean = jnp.sum(density) / (counts[f] * N).astype(f32)
        charges.append((density - mean) * live)
    charge = jnp.concatenate(charges, axis=0)
    blank = jnp.zeros((ENTRIES, N), f32)
    message = jnp.zeros((PEERS, 128), f32)
    for z in range(2):
        padded = jnp.concatenate([charge if i == z else blank for i in range(8)], axis=0)
        rows = slice(z * PEERS, (z + 1) * PEERS)
        message = message + dot3((table_z[0, rows, :], table_z[1, rows, :]), split(padded), NT)
    lane = lax.broadcasted_iota(jnp.int32, (1, 128), 1)
    label = jnp.zeros((1, 128), f32)
    for e in range(ENTRIES):
        label = jnp.where(lane == 2 * ENTRIES + e, line_index(ids, counts, e).astype(f32), label)
    send[pl.ds(8, PEERS, stride=MSG), :] = message + label


def exchange_chunks(parts):
    chunk = lax.broadcasted_iota(jnp.int32, (8, 128), 1) >> 5
    results = []
    for j in range(4):
        total = None
        for i in range(4):
            moved = parts[i] if i == j else pltpu.roll(parts[i], ((i - j) % 4) * 32, 1)
            total = moved if total is None else jnp.where(chunk == i, moved, total)
        results.append(total)
    return results


def solve_kernel(
    arrived, table, table_y, table_yt, eigen, eigen_z, send, plane, wanted_x, placed,
):
    labels = arrived[pl.ds(8, PEERS, stride=MSG), :]
    turned = labels.T
    index = labels.astype(jnp.int32)
    index_t = turned.astype(jnp.int32)
    plane_x = index >> 8
    cell_y = index_t & 255
    row_y = ((cell_y & 15) << 4) + (cell_y >> 4)
    lane = lax.broadcasted_iota(jnp.int32, (PEERS, N), 1)
    sub = lax.broadcasted_iota(jnp.int32, (N, PEERS), 0)
    for e in range(ENTRIES):
        line = 2 * ENTRIES + e
        wanted_x[e * PEERS : (e + 1) * PEERS, :] = (
            (plane_x[:, line : line + 1] == lane).astype(f32).astype(bf16)
        )
        here = row_y[line : line + 1, :] == sub
        for z in range(2):
            value = turned[z * ENTRIES + e : z * ENTRIES + e + 1, :]
            high = value.astype(bf16).astype(f32)
            for part, piece in enumerate((high, value - high)):
                placed[
                    (2 * z + part) * N : (2 * z + part + 1) * N, e * PEERS : (e + 1) * PEERS
                ] = jnp.where(here, piece, 0.0).astype(bf16)
    gathered = dot(placed[...], wanted_x[...])
    for z in range(2):
        for hi in range(2):
            for half in range(2):
                for g in range(4):
                    base = (hi * 4 * OWNERS + half * 8) * MSG + z * 4 + g
                    parts = exchange_chunks(
                        [
                            arrived[pl.ds(base + i * OWNERS * MSG, 8, stride=MSG), :]
                            for i in range(4)
                        ]
                    )
                    for i in range(4):
                        row = z * N + (g * 4 + i) * OWNERS + half * 8
                        plane[row : row + 8, hi * 128 : (hi + 1) * 128] = parts[i]
    table_x = (table[0], table[1])
    forward = (table_y[0], table_y[1])
    backward = (table_yt[0], table_yt[1])
    source = jnp.concatenate(
        [
            gathered[2 * z * N : (2 * z + 1) * N]
            + gathered[(2 * z + 1) * N : (2 * z + 2) * N]
            - plane[z * N : (z + 1) * N, :]
            for z in range(2)
        ],
        axis=0,
    )
    along_x = dot3(split(source), table_x)
    for z in range(2):
        modes = dot3(forward, split(along_x[z * N : (z + 1) * N]))
        modes = modes / (eigen[...] + eigen_z[z])
        plane[z * N : (z + 1) * N, :] = dot3(backward, split(modes))
    plane[...] = dot3(split(plane[...]), table_x)
    for z in range(2):
        for hi in range(2):
            for half in range(2):
                for g in range(4):
                    base = (hi * 4 * OWNERS + half * 8) * MSG + z * 4 + g
                    parts = []
                    for i in range(4):
                        row = z * N + (g * 4 + i) * OWNERS + half * 8
                        parts.append(plane[row : row + 8, hi * 128 : (hi + 1) * 128])
                    parts = exchange_chunks(parts)
                    for i in range(4):
                        send[pl.ds(base + i * OWNERS * MSG, 8, stride=MSG), :] = parts[i]
    high, low = split(plane[...])
    stacked = jnp.concatenate([high, low], axis=0)
    found = [[], []]
    for e in range(ENTRIES):
        line = 2 * ENTRIES + e
        here = row_y[line : line + 1, :] == sub
        columns = dot(stacked, wanted_x[e * PEERS : (e + 1) * PEERS, :], NT)
        for z in range(2):
            both = columns[z * N : (z + 1) * N] + columns[(2 + z) * N : (3 + z) * N]
            found[z].append(jnp.sum(jnp.where(here, both, 0.0), axis=0, keepdims=True))
    rows = jnp.concatenate(
        found[0] + found[1] + [jnp.zeros((PEERS - 2 * ENTRIES, PEERS), f32)], axis=0
    )
    send[pl.ds(8, PEERS, stride=MSG), :] = rows.T


def cycle_kernel(
    ids, counts, degrees, arrived, table_z, first, first_collocated, basis, kinetic, send,
    held, held_kinetic, sem, field, orbitals, collocated, following, gram, factors, lines,
):
    copies = []
    for f in range(FRAGS):
        for i, (source, target) in enumerate(((basis, held), (kinetic, held_kinetic))):
            copies.append(
                pltpu.make_async_copy(source.at[f], target.at[f], sem.at[2 * f + i])
            )
    for copy in copies:
        copy.start()
    turned = arrived[pl.ds(8, PEERS, stride=MSG), :].T
    values = jnp.zeros((ENTRIES, N), f32)
    for z in range(2):
        rows = slice(z * PEERS, (z + 1) * PEERS)
        values = values + dot3(
            split(turned[z * ENTRIES : (z + 1) * ENTRIES, :]),
            (table_z[0, rows, :], table_z[1, rows, :]),
        )
    for f in range(FRAGS):
        field[f * TILES : (f + 1) * TILES, :] = (
            values[f * TILES : (f + 1) * TILES] * live_rows(counts, f)
        )
    for f in range(FRAGS):
        orbitals[f] = first[f]
        collocated[f] = first_collocated[f]
    for copy in copies:
        copy.wait()

    def apply(f, vector, points):
        weights = jnp.concatenate(
            [field[f * TILES + t : f * TILES + t + 1, :] for t in range(TILES)], axis=1
        )
        weighted = (points * weights).astype(bf16)
        return dot(vector, held_kinetic[f]) + dot(weighted, held[f])

    def step(_, carry):
        for f in range(FRAGS):
            earlier = orbitals[f]
            current = (apply(f, earlier, collocated[f]) - CENTER * earlier.astype(f32)) / HALF
            rounded = current.astype(bf16)
            points = dot(rounded, held[f], NT)
            second = 2.0 * (
                apply(f, rounded, points) - CENTER * rounded.astype(f32)
            ) / HALF - earlier.astype(f32)
            chosen = jnp.where(degrees[f] == 2, second, current)
            following[f] = chosen
            gram[f] = lax.dot_general(
                chosen, chosen, NT, precision=lax.Precision.HIGHEST, preferred_element_type=f32
            )
        inverse_factors(gram, factors)
        for f in range(FRAGS):
            rotated = lax.dot_general(
                factors[f], following[f], NN,
                precision=lax.Precision.HIGHEST, preferred_element_type=f32,
            )
            rounded = rotated.astype(bf16)
            orbitals[f] = rounded
            collocated[f] = dot(rounded, held[f], NT)
        return carry

    lax.fori_loop(0, STEPS, step, 0)
    for f in range(FRAGS):
        density_lines(collocated[f], lines, f)
    send[...] = jnp.full((OWNERS * 8, 128), -1.0, f32)
    line_of = [line_index(ids, counts, e) for e in range(ENTRIES)]
    owner_of = [jnp.where(line >= 0, (line & (N - 1)) >> 4, -1) for line in line_of]
    for e in range(ENTRIES):
        rank = jnp.int32(0)
        for i in range(e):
            rank = rank + jnp.where(owner_of[i] == owner_of[e], 1, 0)
        rank = jnp.minimum(rank, 1)
        local = ((line_of[e] >> 8) & (PLANES - 1)) * ROWS + (line_of[e] & (ROWS - 1))

        @pl.when(line_of[e] >= 0)
        def _():
            base = owner_of[e] * 8
            for half in range(2):
                send[pl.ds(base + rank * 2 + half, 1), :] = lines[
                    e : e + 1, half * 128 : (half + 1) * 128
                ]
            send[pl.ds(base + 4 + rank, 1), :] = jnp.full((1, 128), local.astype(f32))


def potential_kernel(arrived, table_z, potential, modes):
    for z in range(2):
        for g in range(4):
            modes[z * PEERS : (z + 1) * PEERS, g * 128 : (g + 1) * 128] = arrived[
                pl.ds(z * 4 + g, PEERS, stride=MSG), :
            ]
    values = dot3(split(modes[...]), (table_z[0], table_z[1]), TN)
    for y in range(ROWS):
        potential[:, y, :] = values[y * PLANES : (y + 1) * PLANES]


def density_kernel(arrived, density):
    lane = lax.broadcasted_iota(jnp.int32, (OWNERS, CELLS), 1)
    masks, values = [], []
    for slot in range(2):
        index = arrived[pl.ds(4 + slot, OWNERS, stride=8), :].astype(jnp.int32)
        masks.append(
            (jnp.concatenate([index] * (CELLS // 128), axis=1) == lane).astype(f32)
        )
        values.append(
            jnp.concatenate(
                [arrived[pl.ds(slot * 2 + half, OWNERS, stride=8), :] for half in range(2)],
                axis=1,
            )
        )
    mask = jnp.concatenate(masks, axis=0).astype(bf16)
    parts = split3(jnp.concatenate(values, axis=0))
    density[...] = dot(mask, parts[0], TN) + (dot(mask, parts[1], TN) + dot(mask, parts[2], TN))


VM = pl.BlockSpec(memory_space=pltpu.VMEM)
SM = pl.BlockSpec(memory_space=pltpu.SMEM)
ANY = pl.BlockSpec(memory_space=pl.ANY)


def call(kernel, name, in_specs, shapes, scratch, operands, flops=0, limit=40):
    outs = [jax.ShapeDtypeStruct(shape, dtype) for shape, dtype in shapes]
    single = len(outs) == 1
    return pl.pallas_call(
        kernel,
        out_shape=outs[0] if single else outs,
        in_specs=in_specs,
        out_specs=VM if single else [VM] * len(outs),
        scratch_shapes=scratch,
        name=name,
        cost_estimate=pl.CostEstimate(flops=flops, bytes_accessed=1 << 20, transcendentals=0),
        compiler_params=pltpu.CompilerParams(vmem_limit_bytes=limit << 20),
    )(*operands)


def trade(message):
    packed = message.reshape(PEERS, MSG, 1, 128)
    return lax.all_to_all(packed, BOTH, 0, 0, tiled=True).reshape(PEERS * MSG, 128)


def shards(kinetic, basis, start_orbitals, background, tile_ids, tile_counts, degrees):
    sines = sine_table()
    eigen = eigen_values()
    order_z = np.concatenate([np.arange(0, N, 2), np.arange(1, N, 2)])
    row = np.arange(N)
    order_y = (row % OWNERS) * ROWS + row // OWNERS
    table_z = halves(sines[order_z])
    table_x = halves(sines)
    table_y = halves(sines[:, order_y])
    table_yt = halves(sines[order_y, :])
    eigen_xy = jnp.asarray((eigen[:, None] + eigen[None, :]).astype(np.float32))
    device = lax.axis_index("frag") * OWNERS + lax.axis_index("grid")
    eigen_z = lax.dynamic_slice(jnp.asarray(eigen.astype(np.float32)), (2 * device,), (2,))

    dma = pltpu.SemaphoreType.DMA
    message_a, first, collocated = call(
        start_kernel, "start",
        [SM, SM, VM, VM, VM, ANY],
        [
            ((PEERS * MSG, 128), f32),
            ((FRAGS, ORB, BASIS), bf16),
            ((FRAGS, ORB, POINTS), f32),
        ],
        [
            pltpu.VMEM((FRAGS, POINTS, BASIS), bf16),
            dma((FRAGS,)),
            pltpu.VMEM((FRAGS, ORB, ORB), f32),
            pltpu.VMEM((FRAGS, ORB, ORB), f32),
            pltpu.VMEM((CELLS, N), bf16),
            pltpu.VMEM((CELLS, N), bf16),
            pltpu.VMEM((ENTRIES, N), f32),
        ],
        (tile_ids, tile_counts, start_orbitals, background, table_z, basis),
        flops=10**10,
    )
    arrived_a = trade(message_a)
    message_b = call(
        solve_kernel, "solve",
        [VM, VM, VM, VM, VM, SM],
        [((PEERS * MSG, 128), f32)],
        [
            pltpu.VMEM((2 * N, N), f32),
            pltpu.VMEM((PEERS * ENTRIES, N), bf16),
            pltpu.VMEM((4 * N, PEERS * ENTRIES), bf16),
        ],
        (arrived_a, table_x, table_y, table_yt, eigen_xy, eigen_z),
        flops=5 * 10**9,
    )
    arrived_b = trade(message_b)
    message_c = call(
        cycle_kernel, "cycle",
        [SM, SM, SM, VM, VM, VM, VM, ANY, ANY],
        [((OWNERS * 8, 128), f32)],
        [
            pltpu.VMEM((FRAGS, POINTS, BASIS), bf16),
            pltpu.VMEM((FRAGS, BASIS, BASIS), bf16),
            dma((2 * FRAGS,)),
            pltpu.VMEM((ENTRIES, N), f32),
            pltpu.VMEM((FRAGS, ORB, BASIS), bf16),
            pltpu.VMEM((FRAGS, ORB, POINTS), f32),
            pltpu.VMEM((FRAGS, ORB, BASIS), f32),
            pltpu.VMEM((FRAGS, ORB, ORB), f32),
            pltpu.VMEM((FRAGS, ORB, ORB), f32),
            pltpu.VMEM((ENTRIES, N), f32),
        ],
        (
            tile_ids, tile_counts, degrees, arrived_b, table_z, first, collocated, basis, kinetic,
        ),
        flops=4 * 10**10,
    )
    arrived_c = lax.all_to_all(
        message_c.reshape(OWNERS, 8, 128), "grid", 0, 0, tiled=True
    ).reshape(OWNERS * 8, 128)
    potential = call(
        potential_kernel, "potential", [VM, VM], [((PLANES, ROWS, N), f32)],
        [pltpu.VMEM((2 * PEERS, CELLS), f32)], (arrived_b, table_z), flops=10**9,
    )
    density = call(
        density_kernel, "density", [VM], [((CELLS, N), f32)], [], (arrived_c,), flops=10**8,
    )
    return potential, density.reshape(PLANES, ROWS, N)


def solution(mesh):
    in_specs = (
        P(BOTH, None, None),
        P(BOTH, None, None),
        P(BOTH, None, None),
        P("frag", "grid", None),
        P(BOTH, None),
        P(BOTH),
        P(BOTH),
    )
    out_specs = (P("frag", "grid", None), P("frag", "grid", None))
    return jax.shard_map(shards, mesh=mesh, in_specs=in_specs, out_specs=out_specs, check_vma=False)
```

```python
import jax
import jax.numpy as jnp
import ml_dtypes
import numpy as np
from jax import lax
from jax.experimental import pallas as pl
from jax.experimental.pallas import tpu as pltpu
from jax.sharding import PartitionSpec as P

f32 = jnp.float32
bf16 = jnp.bfloat16

STEPS = 2
CENTER = 5.0
HALF = 4.0
FRAGS = 2
TILES = 8
ENTRIES = FRAGS * TILES
N = 256
GROUPS = 8
OWNERS = 16
PEERS = GROUPS * OWNERS
PLANES = N // GROUPS
ROWS = N // OWNERS
CELLS = PLANES * ROWS
ORB = 128
BASIS = 1024
POINTS = TILES * N
MSG = 9
BOTH = ("frag", "grid")

NN = (((1,), (0,)), ((), ()))
NT = (((1,), (1,)), ((), ()))
TN = (((0,), (0,)), ((), ()))


def sine_table():
    index = np.arange(1, N + 1)
    phase = np.outer(index, index) % (2 * (N + 1))
    return np.sqrt(2.0 / (N + 1)) * np.sin(np.pi * phase / (N + 1))


def eigen_values():
    return 4.0 * np.sin(np.pi * np.arange(1, N + 1) / (2.0 * (N + 1))) ** 2


def halves(table):
    table = table.astype(np.float32)
    high = table.astype(ml_dtypes.bfloat16)
    low = (table - high.astype(np.float32)).astype(ml_dtypes.bfloat16)
    return jnp.asarray(np.stack([high, low]))


def dot(a, b, dims=NN):
    return lax.dot_general(a, b, dims, preferred_element_type=f32)


def split(x):
    high = x.astype(bf16)
    return high, (x - high.astype(f32)).astype(bf16)


def split3(x):
    high = x.astype(bf16)
    rest = x - high.astype(f32)
    middle = rest.astype(bf16)
    return high, middle, (rest - middle.astype(f32)).astype(bf16)


def dot3(a, b, dims=NN):
    return dot(a[0], b[0], dims) + (dot(a[0], b[1], dims) + dot(a[1], b[0], dims))


def spread(x):
    return jnp.broadcast_to(x, (8, 128))


def tree_sum(terms):
    terms = list(terms)
    while len(terms) > 1:
        terms = [
            terms[i] + terms[i + 1] if i + 1 < len(terms) else terms[i]
            for i in range(0, len(terms), 2)
        ]
    return terms[0]


def lane_columns(x, k):
    return [spread(x[:, k + j : k + j + 1]) for j in range(8)]


def inverse_factors(gram, factors, members):
    lane = lax.broadcasted_iota(jnp.int32, (8, 128), 1)
    sub = lax.broadcasted_iota(jnp.int32, (8, 128), 0)
    size = 32
    blocks = size // 8
    for first in range(0, ORB, size):
        end = first + size
        rows = [
            [gram[f, first + 8 * q : first + 8 * q + 8, :] for q in range(blocks)]
            for f in members
        ]
        done = [[None] * blocks for _ in members]
        pivots = [lane_columns(rows[f][0], first) for f in range(len(members))]
        for p in range(blocks):
            k = first + 8 * p
            last = p == blocks - 1
            inside = (lane >= k) & (lane < k + 8)
            unit = jnp.where(lane - k == sub, 1.0, 0.0)
            panel = [jnp.where(inside, unit, rows[f][p]) for f in range(len(members))]
            ahead = [[] if last else lane_columns(rows[f][p], k + 8) for f in range(len(members))]
            factor = [jnp.zeros((8, 128), f32)] * len(members)
            inverse = [[] for _ in members]
            for j in range(8):
                for f in range(len(members)):
                    column = pivots[f]
                    pivot = spread(column[j][j : j + 1, :])
                    inverse[f].append(1.0 / pivot)
                    row = spread(panel[f][j : j + 1, :])
                    factor[f] = jnp.where(sub == j, row * lax.rsqrt(pivot), factor[f])
                    ratio = jnp.where(sub == j, 0.0, column[j]) * inverse[f][j]
                    for i in range(j + 1, 8):
                        column[i] = column[i] - ratio * spread(column[i][j : j + 1, :])
                    for i in range(len(ahead[f])):
                        ahead[f][i] = ahead[f][i] - ratio * spread(ahead[f][i][j : j + 1, :])
                    panel[f] = panel[f] - ratio * row
            for f in range(len(members)):
                factors[members[f], k : k + 8, :] = jnp.where(lane < k + 8, factor[f], 0.0)
                done[f][p] = jnp.where((lane >= k + 8) & (lane < end), 0.0, factor[f])
                if last:
                    continue
                below = rows[f][p + 1]
                solved = [spread(panel[f][i : i + 1, :]) for i in range(8)]
                scaled = [c * r for c, r in zip(lane_columns(below, k), inverse[f])]
                pivots[f] = [
                    c - tree_sum([scaled[i] * spread(ahead[f][j][i : i + 1, :]) for i in range(8)])
                    for j, c in enumerate(lane_columns(below, k + 8))
                ]
                rows[f][p + 1] = jnp.where(inside, 0.0, below) - tree_sum(
                    [c * r for c, r in zip(scaled, solved)]
                )
                solved = [c * r for c, r in zip(solved, inverse[f])]
                for q in range(p + 2, blocks):
                    below = rows[f][q]
                    rows[f][q] = jnp.where(inside, 0.0, below) - tree_sum(
                        [c * r for c, r in zip(lane_columns(below, k), solved)]
                    )
            yield
        if end == ORB:
            continue
        lanes = lax.broadcasted_iota(jnp.int32, (ORB - end, 128), 1)
        passed = (lanes >= first) & (lanes < end)
        for f in range(len(members)):
            high, middle, low = split3(jnp.concatenate(done[f], axis=0))
            left = jnp.concatenate([high, high, middle, middle, high, low], axis=0)
            right = jnp.concatenate([high, middle, high, middle, low, high], axis=0)
            update = dot(left, right, TN)
            gram[members[f], end:, :] = jnp.where(passed, 0.0, gram[members[f], end:, :]) - update[end:, :]


def run(*works):
    works = list(works)
    while works:
        for work in tuple(works):
            if next(work, works) is works:
                works.remove(work)


def line_index(ids, counts, e):
    f, t = divmod(e, TILES)
    return jnp.where(t < counts[f], ids[f, t], -1)


def live_rows(counts, f):
    slot = lax.broadcasted_iota(jnp.int32, (TILES, N), 0)
    return (slot < counts[f]).astype(f32)


def density_lines(values, lines, f):
    row = 2.0 * jnp.sum(values * values, axis=0, keepdims=True)
    for t in range(TILES):
        lines[f * TILES + t : f * TILES + t + 1, :] = row[:, t * N : (t + 1) * N]


def start_kernel(
    ids, counts, start, ground, table_z, basis, send, orbitals,
    held, sem, gram, factors, lines,
):
    copies = [pltpu.make_async_copy(basis.at[f], held.at[f], sem.at[f]) for f in range(FRAGS)]
    for copy in copies:
        copy.start()
    eye = (
        lax.broadcasted_iota(jnp.int32, (ORB, ORB), 0)
        == lax.broadcasted_iota(jnp.int32, (ORB, ORB), 1)
    ).astype(f32).astype(bf16)
    turned = []
    for f in range(FRAGS):
        across = dot(eye, start[f], NT).astype(bf16)
        turned.append(across)
        gram[f] = dot(across, across, NT)

    def ground_modes():
        for z in range(2):
            rows = slice(z * PEERS, (z + 1) * PEERS)
            for g in range(4):
                values = split(ground[g * 128 : (g + 1) * 128, :])
                send[pl.ds(z * 4 + g, PEERS, stride=MSG), :] = dot3(
                    (table_z[0, rows, :], table_z[1, rows, :]), values, NT
                )
                yield

    run(inverse_factors(gram, factors, (0, 1)), ground_modes())
    charges = []
    for f in range(FRAGS):
        parts = split3(factors[f])
        rotated = dot(parts[0], turned[f]) + (dot(parts[1], turned[f]) + dot(parts[2], turned[f]))
        rounded = rotated.astype(bf16)
        orbitals[f] = rounded
        copies[f].wait()
        density_lines(dot(rounded, held[f], NT), lines, f)
        live = live_rows(counts, f)
        density = lines[f * TILES : (f + 1) * TILES, :] * live
        mean = jnp.sum(density) / (counts[f] * N).astype(f32)
        charges.append((density - mean) * live)
    charge = jnp.concatenate(charges, axis=0)
    blank = jnp.zeros((ENTRIES, N), f32)
    message = jnp.zeros((PEERS, 128), f32)
    for z in range(2):
        padded = jnp.concatenate([charge if i == z else blank for i in range(8)], axis=0)
        rows = slice(z * PEERS, (z + 1) * PEERS)
        message = message + dot3((table_z[0, rows, :], table_z[1, rows, :]), split(padded), NT)
    lane = lax.broadcasted_iota(jnp.int32, (1, 128), 1)
    label = jnp.zeros((1, 128), f32)
    for e in range(ENTRIES):
        label = jnp.where(lane == 2 * ENTRIES + e, line_index(ids, counts, e).astype(f32), label)
    send[pl.ds(8, PEERS, stride=MSG), :] = message + label


def exchange_chunks(parts):
    place = lax.broadcasted_iota(jnp.int32, (8, 128), 1) >> 4
    moved = [parts[0]] + [pltpu.roll(parts[i], 16 * i, 1) for i in range(1, 8)]
    results = []
    for j in range(8):
        total = moved[0]
        for i in range(1, 8):
            total = jnp.where(place == (i + j) % 8, moved[i], total)
        results.append(total if j == 0 else pltpu.roll(total, 128 - 16 * j, 1))
    return results


def turn_kernel(first, basis, kinetic, turned, collocated, applied):
    vector = first[0]
    across = basis[0].T
    turned[0] = across
    collocated[0] = dot(vector, across)
    applied[0] = dot(vector, kinetic[0])


def line_masks():
    row = lax.broadcasted_iota(jnp.int32, (128, 128), 0)
    lane = lax.broadcasted_iota(jnp.int32, (128, 128), 1)
    repeats = [
        (row == part * ENTRIES + (lane & 15)).astype(f32).astype(bf16) for part in range(3)
    ]
    own = (lane >> 4) == (row & 7)
    group = lax.broadcasted_iota(jnp.int32, (16, 128), 0)
    member = lax.broadcasted_iota(jnp.int32, (16, 128), 1) >> 3
    return repeats, own, (group == member).astype(f32).astype(bf16)


def solve_kernel(
    arrived, table, table_p, table_pt, eigen, eigen_z, send, plane, wanted,
):
    repeats, own, members = line_masks()
    labels = arrived[pl.ds(8, PEERS, stride=MSG), :]
    index = labels.astype(jnp.int32)
    plane_x = jnp.where(index < 0, 2 * PLANES, (index >> 8) & (PLANES - 1))
    cell_y = index & (N - 1)
    high, low = split(labels)
    both = jnp.concatenate(repeats[:2], axis=1)
    spread_high, spread_low = dot(high, both), dot(low, both)
    pieces = [
        spread_high[:, :128],
        spread_low[:, :128],
        spread_high[:, 128:],
        spread_low[:, 128:],
        dot(plane_x.astype(f32).astype(bf16), repeats[2]),
        dot(cell_y.astype(f32).astype(bf16), repeats[2]),
    ]
    masked = jnp.concatenate([jnp.where(own, piece, 0.0) for piece in pieces], axis=1)
    grouped = dot(members, masked.astype(bf16))

    def line_row(fq, part):
        lanes = slice(part * 128, (part + 1) * 128)
        return jnp.concatenate(
            [grouped[2 * fq + half : 2 * fq + half + 1, lanes] for half in range(2)], axis=1
        )

    sub_x = lax.broadcasted_iota(jnp.int32, (PLANES, N), 0).astype(f32)
    sub_y = lax.broadcasted_iota(jnp.int32, (N, N), 0).astype(f32)
    here = []
    for fq in range(GROUPS):
        wanted[fq] = (line_row(fq, 5) == sub_y).astype(f32).astype(bf16)
        here.append(line_row(fq, 4) == sub_x)
        values = jnp.concatenate(
            [jnp.where(here[fq], line_row(fq, part), 0.0) for part in range(4)], axis=0
        )
        placed = dot(values.astype(bf16), wanted[fq], NT)
        for z in range(2):
            base = z * 2 * PLANES
            total = placed[base : base + PLANES] + placed[base + PLANES : base + 2 * PLANES]
            for half in range(2):
                plane[pl.ds((z * 2 + half) * N + fq, PLANES, stride=GROUPS), :] = total[
                    :, half * 128 : (half + 1) * 128
                ]
    chunks = [(z, half, g) for z in range(2) for half in range(2) for g in range(4)]
    for z, half, g in chunks:
        parts = exchange_chunks(
            [
                arrived[pl.ds((half * 8 + i) * MSG + z * 4 + g, 8, stride=OWNERS * MSG), :]
                for i in range(8)
            ]
        )
        for i in range(8):
            row = (z * 2 + half) * N + (g * 8 + i) * 8
            plane[row : row + 8, :] = plane[row : row + 8, :] - parts[i]
    table_y = (table[0], table[1])
    forward = (table_p[0], table_p[1])
    backward = (table_pt[0], table_pt[1])
    source = jnp.concatenate(
        [
            jnp.concatenate([plane[z * 2 * N + half * N :][:N] for half in range(2)], axis=1)
            for z in range(2)
        ],
        axis=0,
    )
    along_y = dot3(split(source), table_y)
    modes = []
    for z in range(2):
        mode = dot3(forward, split(along_y[z * N : (z + 1) * N])) / (eigen[...] + eigen_z[z])
        modes.append(dot3(backward, split(mode)))
    values = dot3(split(jnp.concatenate(modes, axis=0)), table_y)
    for z in range(2):
        for half in range(2):
            plane[(z * 2 + half) * N : (z * 2 + half + 1) * N, :] = values[
                z * N : (z + 1) * N, half * 128 : (half + 1) * 128
            ]
    for z, half, g in chunks:
        base = (z * 2 + half) * N + g * 64
        parts = exchange_chunks([plane[base + 8 * i : base + 8 * i + 8, :] for i in range(8)])
        for i in range(8):
            send[pl.ds((half * 8 + i) * MSG + z * 4 + g, 8, stride=OWNERS * MSG), :] = parts[i]
    found = [[], []]
    for fq in range(GROUPS):
        stack = []
        for z in range(2):
            rows = jnp.concatenate(
                [
                    plane[pl.ds((z * 2 + half) * N + fq, PLANES, stride=GROUPS), :]
                    for half in range(2)
                ],
                axis=1,
            )
            stack.extend(split(rows))
        columns = dot(jnp.concatenate(stack, axis=0), wanted[fq])
        for z in range(2):
            base = z * 2 * PLANES
            total = columns[base : base + PLANES] + columns[base + PLANES : base + 2 * PLANES]
            line = jnp.sum(jnp.where(here[fq], total, 0.0), axis=0, keepdims=True)
            found[z].extend([line[:, :128], line[:, 128:]])
    reply = jnp.zeros((PEERS, 128), f32)
    for z in range(2):
        for piece in split(jnp.concatenate(found[z], axis=0)):
            spread_lines = jnp.where(own, dot(members, piece, TN), 0.0)
            reply = reply + dot(spread_lines.astype(bf16), repeats[z], NT)
    send[pl.ds(8, PEERS, stride=MSG), :] = reply


def cycle_kernel(
    ids, counts, degrees, arrived, table_z, first, first_collocated, first_applied,
    basis, turned, kinetic, send,
    held, held_turned, held_kinetic, sem, field, orbitals, weighted, following, gram, factors,
    lines,
):
    copies = []
    for f in range(FRAGS):
        copies.append(
            [
                pltpu.make_async_copy(source.at[f], target.at[f], sem.at[3 * f + i])
                for i, (source, target) in enumerate(
                    ((basis, held), (turned, held_turned), (kinetic, held_kinetic))
                )
            ]
        )
    for three in copies:
        for copy in three:
            copy.start()
    spectrum = arrived[pl.ds(8, PEERS, stride=MSG), :].T
    values = jnp.zeros((ENTRIES, N), f32)
    for z in range(2):
        rows = slice(z * PEERS, (z + 1) * PEERS)
        values = values + dot3(
            split(spectrum[z * ENTRIES : (z + 1) * ENTRIES, :]),
            (table_z[0, rows, :], table_z[1, rows, :]),
        )
    for f in range(FRAGS):
        field[f * TILES : (f + 1) * TILES, :] = (
            values[f * TILES : (f + 1) * TILES] * live_rows(counts, f)
        )

    wide = 2 * N
    parts = BASIS // N

    def weigh(f, part, points):
        tile = f * TILES + 2 * part
        weights = jnp.concatenate([field[tile + t : tile + t + 1, :] for t in range(2)], axis=1)
        weighted[f, :, part * wide : (part + 1) * wide] = (points * weights).astype(bf16)

    def to_grid(f, vector):
        for part in range(POINTS // wide):
            weigh(f, part, dot(vector, held_turned[f, :, part * wide : (part + 1) * wide]))
            yield

    def filtered(f, step):
        if step == 0:
            orbitals[f] = first[f]
            copies[f][0].wait()
            for part in range(POINTS // wide):
                weigh(f, part, first_collocated[f, :, part * wide : (part + 1) * wide])
                yield
        else:
            yield from to_grid(f, orbitals[f])
        tiles = [slice(part * N, (part + 1) * N) for part in range(parts)]
        for tile in tiles:
            earlier = orbitals[f, :, tile].astype(f32)
            if step == 0:
                local = first_applied[f, :, tile]
            else:
                local = dot(orbitals[f], held_kinetic[f, :, tile])
            product = local + dot(weighted[f], held[f, :, tile])
            following[f, :, tile] = (product - CENTER * earlier) / HALF
            yield
        vector = following[f].astype(bf16)
        if step == 0:
            copies[f][1].wait()
            copies[f][2].wait()
        yield from to_grid(f, vector)
        total = jnp.zeros((ORB, ORB), f32)
        for tile in tiles:
            earlier = orbitals[f, :, tile].astype(f32)
            product = dot(vector, held_kinetic[f, :, tile]) + dot(weighted[f], held[f, :, tile])
            second = (
                2.0 * (product - CENTER * vector[:, tile].astype(f32)) / HALF - earlier
            )
            chosen = jnp.where(degrees[f] == 2, second, following[f, :, tile])
            following[f, :, tile] = chosen
            yield
            total = total + lax.dot_general(
                chosen, chosen, NT, precision=lax.Precision.HIGHEST, preferred_element_type=f32
            )
            yield
        gram[f] = total

    def rotated(f):
        for part in range(parts):
            tile = slice(part * N, (part + 1) * N)
            orbitals[f, :, tile] = lax.dot_general(
                factors[f], following[f, :, tile], NN,
                precision=lax.Precision.HIGHEST, preferred_element_type=f32,
            ).astype(bf16)
            yield

    def new_density(f):
        for part in range(POINTS // wide):
            values = dot(orbitals[f], held_turned[f, :, part * wide : (part + 1) * wide])
            row = 2.0 * jnp.sum(values * values, axis=0, keepdims=True)
            for t in range(2):
                line = f * TILES + 2 * part + t
                lines[line : line + 1, :] = row[:, t * N : (t + 1) * N]
            yield

    def chain(*works):
        for work in works:
            yield from work

    run(filtered(0, 0))
    for step in range(STEPS):
        run(inverse_factors(gram, factors, (0,)), filtered(1, step))
        if step < STEPS - 1:
            follow = chain(rotated(0), filtered(0, step + 1))
        else:
            follow = chain(rotated(0), new_density(0))
        run(inverse_factors(gram, factors, (1,)), follow)
        run(rotated(1))
    run(new_density(1))
    send[...] = jnp.full((OWNERS * 8, 128), -1.0, f32)
    line_of = [line_index(ids, counts, e) for e in range(ENTRIES)]
    owner_of = [jnp.where(line >= 0, (line & (N - 1)) >> 4, -1) for line in line_of]
    for e in range(ENTRIES):
        rank = jnp.int32(0)
        for i in range(e):
            rank = rank + jnp.where(owner_of[i] == owner_of[e], 1, 0)
        rank = jnp.minimum(rank, 1)
        local = ((line_of[e] >> 8) & (PLANES - 1)) * ROWS + (line_of[e] & (ROWS - 1))

        @pl.when(line_of[e] >= 0)
        def _():
            base = owner_of[e] * 8
            for half in range(2):
                send[pl.ds(base + rank * 2 + half, 1), :] = lines[
                    e : e + 1, half * 128 : (half + 1) * 128
                ]
            send[pl.ds(base + 4 + rank, 1), :] = jnp.full((1, 128), local.astype(f32))


def potential_kernel(arrived, table_z, potential, modes):
    for z in range(2):
        for g in range(4):
            modes[z * PEERS : (z + 1) * PEERS, g * 128 : (g + 1) * 128] = arrived[
                pl.ds(z * 4 + g, PEERS, stride=MSG), :
            ]
    potential[...] = dot3(split(modes[...]), (table_z[0], table_z[1]), TN)


def density_kernel(arrived, density):
    lane = lax.broadcasted_iota(jnp.int32, (OWNERS, CELLS), 1)
    masks, values = [], []
    for slot in range(2):
        index = arrived[pl.ds(4 + slot, OWNERS, stride=8), :].astype(jnp.int32)
        masks.append(
            (jnp.concatenate([index] * (CELLS // 128), axis=1) == lane).astype(f32)
        )
        values.append(
            jnp.concatenate(
                [arrived[pl.ds(slot * 2 + half, OWNERS, stride=8), :] for half in range(2)],
                axis=1,
            )
        )
    mask = jnp.concatenate(masks, axis=0).astype(bf16)
    parts = split3(jnp.concatenate(values, axis=0))
    density[...] = dot(mask, parts[0], TN) + (dot(mask, parts[1], TN) + dot(mask, parts[2], TN))


VM = pl.BlockSpec(memory_space=pltpu.VMEM)
SM = pl.BlockSpec(memory_space=pltpu.SMEM)
ANY = pl.BlockSpec(memory_space=pl.ANY)


def call(kernel, name, in_specs, shapes, scratch, operands, flops=0, limit=40):
    outs = [jax.ShapeDtypeStruct(shape, dtype) for shape, dtype in shapes]
    single = len(outs) == 1
    return pl.pallas_call(
        kernel,
        out_shape=outs[0] if single else outs,
        in_specs=in_specs,
        out_specs=VM if single else [VM] * len(outs),
        scratch_shapes=scratch,
        name=name,
        cost_estimate=pl.CostEstimate(flops=flops, bytes_accessed=1 << 20, transcendentals=0),
        compiler_params=pltpu.CompilerParams(vmem_limit_bytes=limit << 20),
    )(*operands)


def trade(message):
    packed = message.reshape(PEERS, MSG, 1, 128)
    return lax.all_to_all(packed, BOTH, 0, 0, tiled=True).reshape(PEERS * MSG, 128)


def shards(kinetic, basis, start_orbitals, background, tile_ids, tile_counts, degrees):
    sines = sine_table()
    eigen = eigen_values()
    order_z = np.concatenate([np.arange(0, N, 2), np.arange(1, N, 2)])
    row = np.arange(N)
    order_x = (row % GROUPS) * PLANES + row // GROUPS
    table_z = halves(sines[order_z])
    table_y = halves(sines)
    table_p = halves(sines[:, order_x])
    table_pt = halves(sines[order_x, :])
    eigen_xy = jnp.asarray((eigen[:, None] + eigen[None, :]).astype(np.float32))
    device = lax.axis_index("frag") * OWNERS + lax.axis_index("grid")
    eigen_z = lax.dynamic_slice(jnp.asarray(eigen.astype(np.float32)), (2 * device,), (2,))

    dma = pltpu.SemaphoreType.DMA
    square = pltpu.VMEM((FRAGS, ORB, ORB), f32)
    message_a, first = call(
        start_kernel, "start",
        [SM, SM, VM, VM, VM, ANY],
        [((PEERS * MSG, 128), f32), ((FRAGS, ORB, BASIS), bf16)],
        [
            pltpu.VMEM((FRAGS, POINTS, BASIS), bf16),
            dma((FRAGS,)),
            square,
            square,
            pltpu.VMEM((ENTRIES, N), f32),
        ],
        (tile_ids, tile_counts, start_orbitals, background.reshape(CELLS, N), table_z, basis),
        flops=10**10, limit=60,
    )
    arrived_a = trade(message_a)
    part = POINTS // 4
    turned, collocated, applied = pl.pallas_call(
        turn_kernel,
        grid=(FRAGS, 4),
        out_shape=[
            jax.ShapeDtypeStruct((FRAGS, BASIS, POINTS), bf16),
            jax.ShapeDtypeStruct((FRAGS, ORB, POINTS), f32),
            jax.ShapeDtypeStruct((FRAGS, ORB, BASIS), f32),
        ],
        in_specs=[
            pl.BlockSpec((1, ORB, BASIS), lambda f, i: (f, 0, 0)),
            pl.BlockSpec((1, part, BASIS), lambda f, i: (f, i, 0)),
            pl.BlockSpec((1, BASIS, BASIS // 4), lambda f, i: (f, 0, i)),
        ],
        out_specs=[
            pl.BlockSpec((1, BASIS, part), lambda f, i: (f, 0, i)),
            pl.BlockSpec((1, ORB, part), lambda f, i: (f, 0, i)),
            pl.BlockSpec((1, ORB, BASIS // 4), lambda f, i: (f, 0, i)),
        ],
        name="turn",
        cost_estimate=pl.CostEstimate(flops=10**10, bytes_accessed=24 << 20, transcendentals=0),
        compiler_params=pltpu.CompilerParams(vmem_limit_bytes=60 << 20),
    )(first, basis, kinetic)
    arrived_a, turned, collocated, applied = lax.optimization_barrier(
        (arrived_a, turned, collocated, applied)
    )
    message_b = call(
        solve_kernel, "solve",
        [VM, VM, VM, VM, VM, SM],
        [((PEERS * MSG, 128), f32)],
        [pltpu.VMEM((4 * N, 128), f32), pltpu.VMEM((GROUPS, N, N), bf16)],
        (arrived_a, table_y, table_p, table_pt, eigen_xy, eigen_z),
        flops=5 * 10**9, limit=24,
    )
    arrived_b = trade(message_b)
    message_c = call(
        cycle_kernel, "cycle",
        [SM, SM, SM, VM, VM, VM, VM, VM, ANY, ANY, ANY],
        [((OWNERS * 8, 128), f32)],
        [
            pltpu.VMEM((FRAGS, POINTS, BASIS), bf16),
            pltpu.VMEM((FRAGS, BASIS, POINTS), bf16),
            pltpu.VMEM((FRAGS, BASIS, BASIS), bf16),
            dma((3 * FRAGS,)),
            pltpu.VMEM((ENTRIES, N), f32),
            pltpu.VMEM((FRAGS, ORB, BASIS), bf16),
            pltpu.VMEM((FRAGS, ORB, POINTS), bf16),
            pltpu.VMEM((FRAGS, ORB, BASIS), f32),
            square,
            square,
            pltpu.VMEM((ENTRIES, N), f32),
        ],
        (
            tile_ids, tile_counts, degrees, arrived_b, table_z, first, collocated, applied,
            basis, turned, kinetic,
        ),
        flops=4 * 10**10, limit=40,
    )
    arrived_c = lax.all_to_all(
        message_c.reshape(OWNERS, 8, 128), "grid", 0, 0, tiled=True
    ).reshape(OWNERS * 8, 128)
    potential = call(
        potential_kernel, "potential", [VM, VM], [((CELLS, N), f32)],
        [pltpu.VMEM((2 * PEERS, CELLS), f32)], (arrived_b, table_z), flops=10**9,
    )
    density = call(
        density_kernel, "density", [VM], [((CELLS, N), f32)], [], (arrived_c,), flops=10**8,
    )
    return potential.reshape(PLANES, ROWS, N), density.reshape(PLANES, ROWS, N)


def solution(mesh):
    in_specs = (
        P(BOTH, None, None),
        P(BOTH, None, None),
        P(BOTH, None, None),
        P("frag", "grid", None),
        P(BOTH, None),
        P(BOTH),
        P(BOTH),
    )
    out_specs = (P("frag", "grid", None), P("frag", "grid", None))
    return jax.shard_map(shards, mesh=mesh, in_specs=in_specs, out_specs=out_specs, check_vma=False)
```
